32 devices in a mesh: expert: 4 (over z), fsdp: 2 (over y), tensor: 4 (over x, core).
Axes of the slice: x: 2, y: 2, z: 4, core: 2. Of those that a mesh axis runs over, the one named last changes fastest.
Arguments:
- tokens: bfloat16 [512, 4096], P('expert', 'tensor'), may hold values from -6 to 6
- expert_ids: int32 [512, 2], P('expert'), may hold values from 0 to 3, all different within a row; in each aligned block of 128 rows (0 to 127, 128 to 255, ...) at most 96 rows name the same one
- gate_probs: float32 [512, 2], P('expert'), may hold values from 0.1 to 1
- w_gate: bfloat16 [4, 4096, 14336], P('expert', 'tensor', 'fsdp'), may hold values from -0.09375 to 0.09375
- w_up: bfloat16 [4, 4096, 14336], P('expert', 'tensor', 'fsdp'), may hold values from -0.09375 to 0.09375
- w_down: bfloat16 [4, 14336, 4096], P('expert', 'fsdp', 'tensor'), may hold values from -0.046875 to 0.046875
Outputs:
- mixed: bfloat16 [512, 4096], P('expert', 'tensor')
The draws below stay inside these ranges and needn't reach their ends.
Inputs may be any that keep to these rules, and one draw needn't show every extreme that they name: `expert_ids`: in each aligned block of 128 tokens no expert is named by more than 96 tokens, a bound that some block reaches; a token names two different experts.
All inputs are finite; a program needn't handle non-finite values.
Results may differ from the reference program's by a relative error of at most 0.0049.
Values may be sent and summed in bfloat16 or wider, within the bound.
No kernel may reach another device: no remote copies, remote signals or barrier semaphores. Data moves between devices by JAX's collectives and lax.ppermute only.
A program may use at most 128 MiB of HBM per device.

```python
import math
import jax
import jax.numpy as jnp
import numpy as np
from jax import lax

D = 4096
FF = 14336
TOPK = 2
TOK_DEV = 128
EXPERTS = 4
CAP = 96
TOKENS = 512


def levels(rng, dims, pieces, low, high):
    def one(dim, shards_of):
        steps = jax.random.uniform(jax.random.fold_in(jax.random.fold_in(rng, 6), dim), (shards_of,), jnp.float32, low / len(pieces), high / len(pieces))
        return jnp.repeat(jnp.exp(steps), dims[dim] // shards_of).reshape((-1,) + (1,) * (len(dims) - dim - 1))

    factor_of = one(*pieces[0])
    for cut in pieces[1:]:
        factor_of = factor_of * one(*cut)
    return factor_of


def routed_block(rng, own, number, rows, number_of, top, reach, skew):
    order = jax.random.permutation(rng, number_of)
    crowded, usual = shares(number_of, rows * top, reach, skew, True), shares(number_of, rows * top, reach, skew, False)
    places = jnp.arange(number_of)

    def named(tallies, rotation):
        used = int((tallies > 0).sum())
        fixed = max(1, used // 4)
        moved = fixed + (places - fixed + rotation * (used - fixed)) % max(1, number_of - fixed)
        return jnp.zeros((number_of,), jnp.int32).at[order[jnp.where(places < fixed, places, moved)]].set(jnp.asarray(tallies, jnp.int32))

    tallies = jnp.where(number % 4 == 0, named(crowded, number // 4), named(usual, number - number // 4 - 1))
    mixed = jax.random.permutation(jax.random.fold_in(own, 3), number_of)
    source_of, taker = mixed[0:number_of // 2 * 2:2], mixed[1:number_of // 2 * 2:2]
    room = jnp.minimum(tallies[source_of] - 1, reach - tallies[taker]) // 2
    room = jnp.where((source_of == order[0]) | (taker == order[0]) | (tallies[taker] == 0), 0, jnp.maximum(room, 0))
    moved = jax.random.randint(jax.random.fold_in(own, 4), (number_of // 2,), 0, 1 << 20) % (room + 1)
    tallies = tallies.at[source_of].add(-moved).at[taker].add(moved)
    labels = jnp.searchsorted(jnp.cumsum(tallies), jnp.arange(rows * top), side="right").astype(jnp.int32)
    grid = labels.reshape(top, rows).T
    grid = grid[jax.random.permutation(jax.random.fold_in(own, 1), rows)]
    rotation = jax.random.randint(jax.random.fold_in(own, 2), (rows, 1), 0, top)
    return jnp.take_along_axis(grid, (jnp.arange(top)[None, :] + rotation) % top, axis=1)


def shares(amount, total, bound, skew, full):
    portions = [(1 << 20) // math.isqrt(standing ** skew) + 1 for standing in range(1, amount + 1)]
    largest = bound if full else min(bound, max(-(-total // amount), total * portions[0] // sum(portions)))
    least = 1 if total - largest >= amount - 1 else 0
    given, surplus = [largest] + [least] * (amount - 1), total - largest - least * (amount - 1)
    while surplus > 0:
        candidates = [i for i in range(1, amount) if given[i] < largest] or [i for i in range(1, amount) if given[i] < bound]
        whole, left = sum([portions[i] for i in candidates]), surplus
        for i in candidates:
            addition = min(bound - given[i], max(1, left * portions[i] // whole), surplus)
            given[i] = given[i] + addition
            surplus = surplus - addition
    return np.array(given)


def normal_values(rng, dims, spread, bound, cuts=(), held_as=jnp.bfloat16):
    loudness = levels(rng, dims, cuts, -0.22, 0.18) if cuts else 1.0
    array = jax.random.normal(rng, dims, jnp.float32) * spread * loudness
    return jnp.minimum(jnp.maximum(array, -bound), bound).astype(held_as)


def setup_inputs(seed: int = 0) -> dict:
    key_list = jax.random.split(jax.random.key(seed), 7)
    tokens = normal_values(key_list[0], (TOKENS, D), 1.0, 6.0, ((0, 4), (1, 4)))
    expert_ids_keys = jax.random.split(jax.random.fold_in(key_list[1], 1), TOKENS // TOK_DEV)
    expert_ids_turns = jax.random.permutation(jax.random.fold_in(key_list[1], 3), TOKENS // TOK_DEV)
    expert_ids = jax.vmap(lambda own, number: routed_block(jax.random.fold_in(key_list[1], 2), own, number, TOK_DEV, EXPERTS, TOPK, CAP, 2))(expert_ids_keys, expert_ids_turns).reshape((TOKENS, TOPK))
    gate_probs = jnp.clip(0.1 + 0.9 * jax.random.uniform(key_list[2], (TOKENS, TOPK), jnp.float32) ** levels(key_list[2], (TOKENS, TOPK), ((0, 4),), -0.2, 0.2), 0.1, 1.0)
    w_gate = normal_values(key_list[3], (EXPERTS, D, FF), D ** -0.5, 0.09375, ((0, 4), (1, 4), (2, 2)))
    w_up = normal_values(key_list[4], (EXPERTS, D, FF), D ** -0.5, 0.09375, ((0, 4), (1, 4), (2, 2)))
    w_down = normal_values(key_list[5], (EXPERTS, FF, D), FF ** -0.5, 0.046875, ((0, 4), (1, 2), (2, 4)))
    return dict(tokens=tokens, expert_ids=expert_ids, gate_probs=gate_probs, w_gate=w_gate, w_up=w_up, w_down=w_down)


def expert_apply(operands):
    rows_in, gate_matrix, up_matrix, down_matrix = operands
    gate = jnp.dot(rows_in, gate_matrix, preferred_element_type=jnp.float32)
    up_value = jnp.dot(rows_in, up_matrix, preferred_element_type=jnp.float32)
    hidden = (jax.nn.silu(gate) * up_value).astype(jnp.bfloat16)
    return jnp.dot(hidden, down_matrix, preferred_element_type=jnp.float32)


def reference(tokens, expert_ids, gate_probs, w_gate, w_up, w_down):
    sources = TOKENS // TOK_DEV
    block_ids = expert_ids.reshape(sources, TOK_DEV * TOPK)
    onehot = (block_ids[:, :, None] == jnp.arange(EXPERTS, dtype=jnp.int32)[None, None, :]).astype(jnp.int32)
    slot_rank = jnp.cumsum(onehot, axis=1) - onehot
    slot_index = jnp.sum(slot_rank * onehot, axis=2).astype(jnp.int32)
    row_index = (jnp.arange(sources, dtype=jnp.int32)[:, None] * CAP + slot_index).astype(jnp.int32)
    doubled = jnp.repeat(tokens.reshape(sources, TOK_DEV, D), TOPK, axis=1)
    dispatched = jnp.zeros((EXPERTS, sources * CAP, D), jnp.bfloat16)
    dispatched = dispatched.at[block_ids, row_index].set(doubled)
    expert_out = lax.map(expert_apply, (dispatched, w_gate, w_up, w_down))
    picked = expert_out[block_ids, row_index]
    picked = picked.reshape(sources, TOK_DEV, TOPK, D)
    weights = gate_probs.reshape(sources, TOK_DEV, TOPK, 1)
    mixed = jnp.sum(picked * weights, axis=2)
    return mixed.reshape(TOKENS, D).astype(jnp.bfloat16)
```

```python
import functools

import jax
import jax.numpy as jnp
from jax import lax
from jax.experimental import pallas as pl
from jax.experimental.pallas import tpu as pltpu
from jax.sharding import PartitionSpec as P

F32 = jnp.float32
BF16 = jnp.bfloat16
VMEM_LIMIT = 40 * 1024 * 1024


def xor_swap(value, axis, distance):
    size = lax.axis_size(axis)
    return lax.ppermute(value, axis, [(i, i ^ distance) for i in range(size)])


def bit_reverse(value, bits):
    out = 0
    for _ in range(bits):
        out = out * 2 + value % 2
        value //= 2
    return out


def tile_width(width, options):
    for option in options:
        if width % option == 0:
            return option
    return None


def up_kernel(x_ref, gate_ref, up_ref, keep_ref, send_ref):
    half = keep_ref.shape[1]
    for which, w_ref in enumerate((gate_ref, up_ref)):
        product = jnp.dot(x_ref[...], w_ref[...], preferred_element_type=F32)
        keep_ref[which] = product[:half]
        send_ref[which] = product[half:]


def project_up(rows, w_gate, w_up, start, width):
    count, depth = rows.shape
    half = count // 2
    block = tile_width(width, (512, 256))
    if half % 16 or depth % 128 or block is None or start % block:
        columns = slice(start, start + width)
        product = jnp.stack(
            [jnp.dot(rows, w[:, columns], preferred_element_type=F32) for w in (w_gate, w_up)]
        )
        return product[:, :half], product[:, half:]
    weight_spec = pl.BlockSpec((depth, block), lambda i: (0, start // block + i))
    out_spec = pl.BlockSpec((2, half, block), lambda i: (0, 0, i))
    out_type = jax.ShapeDtypeStruct((2, half, width), F32)
    return pl.pallas_call(
        up_kernel,
        grid=(width // block,),
        in_specs=[pl.BlockSpec((count, depth), lambda i: (0, 0)), weight_spec, weight_spec],
        out_specs=[out_spec, out_spec],
        out_shape=[out_type, out_type],
        compiler_params=pltpu.CompilerParams(vmem_limit_bytes=VMEM_LIMIT),
        cost_estimate=pl.CostEstimate(
            flops=4 * count * depth * width,
            bytes_accessed=4 * depth * width + 8 * count * width,
            transcendentals=0,
        ),
        name="project_up",
    )(rows, w_gate, w_up)


def down_kernel(has_total, *refs):
    if has_total:
        near_ref, far_ref, w_ref, total_ref, out_ref = refs
    else:
        near_ref, far_ref, w_ref, out_ref = refs
    half = near_ref.shape[0]

    @pl.when(pl.program_id(0) == 0)
    def _():
        out_ref[...] = total_ref[...] if has_total else jnp.zeros_like(out_ref)

    hidden = jnp.concatenate([near_ref[...], far_ref[...]], axis=0)
    out_ref[...] += jnp.dot(hidden, w_ref[...], preferred_element_type=F32)


def project_down(near, far, w_down, start, total):
    half, width = near.shape
    depth = w_down.shape[1]
    block = tile_width(width, (512, 256))
    if half % 16 or depth % 128 or block is None or start % block:
        hidden = jnp.concatenate([near, far], axis=0)
        product = jnp.dot(hidden, w_down[start : start + width], preferred_element_type=F32)
        return product if total is None else total + product
    hidden_spec = pl.BlockSpec((half, block), lambda i: (0, i))
    whole = pl.BlockSpec((2 * half, depth), lambda i: (0, 0))
    has_total = total is not None
    return pl.pallas_call(
        functools.partial(down_kernel, has_total),
        grid=(width // block,),
        in_specs=[
            hidden_spec,
            hidden_spec,
            pl.BlockSpec((block, depth), lambda i: (start // block + i, 0)),
        ]
        + [whole] * has_total,
        out_specs=whole,
        out_shape=jax.ShapeDtypeStruct((2 * half, depth), F32),
        compiler_params=pltpu.CompilerParams(vmem_limit_bytes=VMEM_LIMIT),
        cost_estimate=pl.CostEstimate(
            flops=4 * half * depth * width,
            bytes_accessed=2 * depth * width + 4 * half * width,
            transcendentals=0,
        ),
        name="project_down",
    )(near, far, w_down, *([total] * has_total))


def reduce_tile(rows, w_gate, w_up, start, width):
    bits = lax.axis_size("tensor").bit_length() - 1
    keep, send = project_up(rows, w_gate, w_up, start, width)
    for bit in range(bits):
        arrived = xor_swap(send, "tensor", 1 << bit).astype(F32)
        total = keep + arrived
        if bit < bits - 1:
            half = total.shape[1] // 2
            keep, send = total[:, :half], total[:, half:].astype(BF16)
    return (jax.nn.silu(total[0]) * total[1]).astype(BF16)


def gather_tile(share):
    bits = lax.axis_size("tensor").bit_length() - 1
    near = share
    for bit in reversed(range(bits)):
        far = xor_swap(near, "tensor", 1 << bit)
        if bit:
            near = jnp.concatenate([near, far], axis=0)
    return near, far


def body(tokens, expert_ids, gate_probs, w_gate, w_up, w_down):
    tok_rows, feature_part = tokens.shape
    experts = lax.axis_size("expert")
    parts = lax.axis_size("tensor")
    bits = parts.bit_length() - 1
    capacity = 3 * tok_rows // experts
    piece = capacity // parts
    me = lax.axis_index("expert")
    my_part = lax.axis_index("tensor")

    relative = expert_ids ^ me
    names = relative[:, :, None] == jnp.arange(experts, dtype=jnp.int32)[None, None, :]
    named = jnp.any(names, axis=1)
    chance = jnp.sum(jnp.where(names, gate_probs[:, :, None], 0.0), axis=1)
    earlier = jnp.tril(jnp.ones((tok_rows, tok_rows), BF16), -1)
    rank = jnp.dot(earlier, named.astype(BF16), preferred_element_type=F32).astype(jnp.int32)
    place = jnp.where(named, rank, -1).T
    order = jnp.asarray([bit_reverse(j, bits) for j in range(parts)], jnp.int32) ^ my_part
    slots = (order[:, None] * piece + jnp.arange(piece, dtype=jnp.int32)[None, :]).reshape(-1)
    chosen = slots[None, :, None] == place[:, None, :]
    outgoing = jnp.dot(
        chosen.reshape(-1, tok_rows).astype(BF16), tokens, preferred_element_type=F32
    ).astype(BF16)
    outgoing = outgoing.reshape(experts, capacity, feature_part)
    weigh = jnp.where(chosen, chance.T[:, None, :], 0.0)

    arrived = [outgoing[0]] + [xor_swap(outgoing[k], "expert", k) for k in range(1, experts)]
    width_all = w_gate.shape[2]
    groups = [[1], list(range(2, experts)), [0]]
    cuts = [2, 4, 2]
    returned = [None] * experts
    for group, cut in zip(groups, cuts):
        count = len(group)
        rows = jnp.stack([arrived[k] for k in group]).reshape(count, parts, piece, feature_part)
        rows = rows.transpose(1, 0, 2, 3).reshape(-1, feature_part)
        width = width_all // cut
        total = None
        for part in range(cut):
            share = reduce_tile(rows, w_gate[0], w_up[0], part * width, width)
            near, far = gather_tile(share)
            total = project_down(near, far, w_down[0], part * width, total)
        total = total.reshape(parts, count, piece, feature_part).transpose(1, 0, 2, 3)
        total = total.reshape(count, capacity, feature_part)
        for index, k in enumerate(group):
            if k:
                returned[k] = xor_swap(total[index].astype(BF16), "expert", k).astype(F32)
            else:
                returned[k] = total[index]
    back = jnp.concatenate(returned, axis=0)
    mixed = lax.dot_general(
        weigh.reshape(-1, tok_rows),
        back,
        (((0,), (0,)), ((), ())),
        precision=lax.Precision.HIGHEST,
        preferred_element_type=F32,
    )
    size = lax.axis_size("fsdp")
    for bit in range(size.bit_length() - 1):
        mixed = mixed + xor_swap(mixed, "fsdp", 1 << bit)
    return mixed.astype(BF16)


def solution(mesh):
    return jax.shard_map(
        body,
        mesh=mesh,
        in_specs=(
            P("expert", "tensor"),
            P("expert", None),
            P("expert", None),
            P("expert", "tensor", "fsdp"),
            P("expert", "tensor", "fsdp"),
            P("expert", "fsdp", "tensor"),
        ),
        out_specs=P("expert", "tensor"),
        check_vma=False,
    )
```

```python
import functools

import jax
import jax.numpy as jnp
from jax import lax
from jax.experimental import pallas as pl
from jax.experimental.pallas import tpu as pltpu
from jax.sharding import PartitionSpec as P

F32 = jnp.float32
BF16 = jnp.bfloat16
VMEM_LIMIT = 24 * 1024 * 1024
SMALL_LIMIT = 14 * 1024 * 1024
BRIEF = pl.CostEstimate(flops=1, bytes_accessed=1, transcendentals=0)
LONG = pl.CostEstimate(flops=10**11, bytes_accessed=10**8, transcendentals=0)
CUTS = ((1, 3, 4), (4, 3, 1))


def xor_swap(value, axis, distance):
    size = lax.axis_size(axis)
    return lax.ppermute(value, axis, [(i, i ^ distance) for i in range(size)])


def bit_reverse(value, bits):
    out = 0
    for _ in range(bits):
        out = out * 2 + value % 2
        value //= 2
    return out


def tile_width(width, options):
    for option in options:
        if width % option == 0:
            return option
    return None


def up_kernel(start, width, block, x_ref, gate_ref, up_ref, keep_ref, send_ref, weights, products, weight_sems, out_sems):
    half = x_ref.shape[0] // 2
    chunks = width // block
    depth = weights.shape[0]
    sources = (gate_ref, up_ref)

    def fetch(chunk, slot, which):
        columns = pl.ds(pl.multiple_of(start + chunk * block, block), block)
        return pltpu.make_async_copy(
            sources[which].at[:, columns], weights.at[slot, which], weight_sems.at[slot, which]
        )

    def store(chunk, slot, which, part):
        columns = pl.ds(pl.multiple_of(chunk * block, block), block)
        target = (keep_ref, send_ref)[part]
        return pltpu.make_async_copy(
            products.at[slot, which, pl.ds(part * half, half)],
            target.at[which, :, columns],
            out_sems.at[slot, which, part],
        )

    for chunk in range(min(depth, chunks)):
        for which in range(2):
            fetch(chunk, chunk, which).start()

    def step(chunk, carry):
        slot = lax.rem(chunk, depth)
        out_slot = lax.rem(chunk, 2)
        for which in range(2):
            fetch(chunk, slot, which).wait()

            @pl.when(chunk >= 2)
            def _():
                for part in range(2):
                    store(chunk - 2, out_slot, which, part).wait()

            products[out_slot, which] = jnp.dot(
                x_ref[...], weights[slot, which], preferred_element_type=F32
            )
            for part in range(2):
                store(chunk, out_slot, which, part).start()

            @pl.when(chunk + depth < chunks)
            def _():
                fetch(chunk + depth, slot, which).start()

        return carry

    lax.fori_loop(0, chunks, step, 0)
    for chunk in range(max(0, chunks - 2), chunks):
        for which in range(2):
            for part in range(2):
                store(chunk, chunk % 2, which, part).wait()


def project_up(rows, w_gate, w_up, start, width):
    count, depth = rows.shape
    half = count // 2
    block = tile_width(width, (896, 512, 256))
    if half % 8 or count % 16 or depth % 128 or block is None or start % block:
        columns = slice(start, start + width)
        product = jnp.stack(
            [jnp.dot(rows, w[:, columns], preferred_element_type=F32) for w in (w_gate, w_up)]
        )
        return product[:, :half], product[:, half:]
    slots = min(4, width // block)
    anywhere = pl.BlockSpec(memory_space=pl.ANY)
    hbm = pl.BlockSpec(memory_space=pltpu.HBM)
    out_type = jax.ShapeDtypeStruct((2, half, width), F32)
    return pl.pallas_call(
        functools.partial(up_kernel, start, width, block),
        in_specs=[pl.BlockSpec(memory_space=pltpu.VMEM), hbm, hbm],
        out_specs=[anywhere, anywhere],
        out_shape=[out_type, out_type],
        scratch_shapes=[
            pltpu.VMEM((slots, 2, depth, block), BF16),
            pltpu.VMEM((2, 2, count, block), F32),
            pltpu.SemaphoreType.DMA((slots, 2)),
            pltpu.SemaphoreType.DMA((2, 2, 2)),
        ],
        compiler_params=pltpu.CompilerParams(vmem_limit_bytes=VMEM_LIMIT),
        cost_estimate=LONG,
        name="project_up",
    )(rows, in_hbm(w_gate), in_hbm(w_up))


def down_kernel(start, width, block, count, has_total, *refs):
    pieces, w_ref = refs[:count], refs[count]
    out_ref, weights, sems = refs[-3:]
    chunks = width // block
    depth = weights.shape[0]

    def fetch(chunk, slot):
        rows = pl.ds(pl.multiple_of(start + chunk * block, block), block)
        return pltpu.make_async_copy(w_ref.at[rows], weights.at[slot], sems.at[slot])

    for chunk in range(min(depth, chunks)):
        fetch(chunk, chunk).start()
    out_ref[...] = refs[count + 1][...] if has_total else jnp.zeros_like(out_ref)

    def step(chunk, carry):
        slot = lax.rem(chunk, depth)
        fetch(chunk, slot).wait()
        columns = pl.ds(pl.multiple_of(chunk * block, block), block)
        hidden = jnp.concatenate([piece[:, columns] for piece in pieces], axis=0)
        out_ref[...] += jnp.dot(hidden, weights[slot], preferred_element_type=F32)

        @pl.when(chunk + depth < chunks)
        def _():
            fetch(chunk + depth, slot).start()

        return carry

    lax.fori_loop(0, chunks, step, 0)


def project_down(pieces, w_down, start, total):
    rows, width = pieces[0].shape
    count = len(pieces)
    depth = w_down.shape[1]
    block = tile_width(width, (896, 512, 256))
    if rows % 16 or depth % 128 or block is None or start % block:
        hidden = jnp.concatenate(pieces, axis=0)
        product = jnp.dot(hidden, w_down[start : start + width], preferred_element_type=F32)
        return product if total is None else total + product
    slots = min(6, width // block)
    vmem = pl.BlockSpec(memory_space=pltpu.VMEM)
    has_total = total is not None
    return pl.pallas_call(
        functools.partial(down_kernel, start, width, block, count, has_total),
        in_specs=[vmem] * count + [pl.BlockSpec(memory_space=pltpu.HBM)] + [vmem] * has_total,
        out_specs=vmem,
        out_shape=jax.ShapeDtypeStruct((count * rows, depth), F32),
        scratch_shapes=[
            pltpu.VMEM((slots, block, depth), BF16),
            pltpu.SemaphoreType.DMA((slots,)),
        ],
        compiler_params=pltpu.CompilerParams(vmem_limit_bytes=VMEM_LIMIT),
        cost_estimate=BRIEF,
        name="project_down",
    )(*pieces, in_hbm(w_down), *([total] * has_total))


def fold_kernel(keep_ref, arrived_ref, kept_ref, send_ref):
    half, width = kept_ref.shape[1:]
    block = tile_width(width, (896, 512, 256))

    def step(chunk, carry):
        columns = pl.ds(pl.multiple_of(chunk * block, block), block)
        for which in range(2):
            total = keep_ref[which, :, columns] + arrived_ref[which, :, columns]
            kept_ref[which, :, columns] = total[:half]
            send_ref[which, :, columns] = total[half:].astype(BF16)
        return carry

    lax.fori_loop(0, width // block, step, 0)


def fold(keep, arrived):
    rows, width = keep.shape[1:]
    half = rows // 2
    if half % 8 or tile_width(width, (896, 512, 256)) is None or arrived.dtype != F32:
        total = keep + arrived.astype(F32)
        return total[:, :half], total[:, half:].astype(BF16)
    vmem = pl.BlockSpec(memory_space=pltpu.VMEM)
    return pl.pallas_call(
        fold_kernel,
        in_specs=[vmem, vmem],
        out_specs=[vmem, vmem],
        out_shape=[
            jax.ShapeDtypeStruct((2, half, width), F32),
            jax.ShapeDtypeStruct((2, half, width), BF16),
        ],
        compiler_params=pltpu.CompilerParams(vmem_limit_bytes=SMALL_LIMIT),
        cost_estimate=BRIEF,
        name="fold",
    )(keep, arrived)


def hidden_kernel(keep_ref, arrived_ref, out_ref):
    width = out_ref.shape[1]
    block = tile_width(width, (896, 512, 256))

    def step(chunk, carry):
        columns = pl.ds(pl.multiple_of(chunk * block, block), block)
        gate, up = [keep_ref[i, :, columns] + arrived_ref[i, :, columns].astype(F32) for i in range(2)]
        out_ref[:, columns] = (gate / (1.0 + jnp.exp(-gate)) * up).astype(BF16)
        return carry

    lax.fori_loop(0, width // block, step, 0)


def hidden(keep, arrived):
    rows, width = keep.shape[1:]
    if rows % 8 or tile_width(width, (896, 512, 256)) is None:
        total = keep + arrived.astype(F32)
        return (jax.nn.silu(total[0]) * total[1]).astype(BF16)
    vmem = pl.BlockSpec(memory_space=pltpu.VMEM)
    return pl.pallas_call(
        hidden_kernel,
        in_specs=[vmem, vmem],
        out_specs=vmem,
        out_shape=jax.ShapeDtypeStruct((rows, width), BF16),
        compiler_params=pltpu.CompilerParams(vmem_limit_bytes=SMALL_LIMIT),
        cost_estimate=BRIEF,
        name="hidden",
    )(keep, arrived)


def in_hbm(value):
    return pltpu.with_memory_space_constraint(value, pltpu.HBM)


def after(token, *values):
    if token is None:
        return values
    return lax.optimization_barrier((*values, token))[:-1]


def tensor_bits():
    return lax.axis_size("tensor").bit_length() - 1


class Tile:
    def __init__(self, group, start, width, last):
        self.group, self.start, self.width, self.last = group, start, width, last
        self.previous = None
        self.out = None


def order_of(count):
    steps = []
    for step in range(count + 4):
        for kind, behind in (("fold", 2), ("hidden", 3), ("up", 0), ("down", 4)):
            if 0 <= step - behind < count:
                steps.append((kind, step - behind))
    return steps


def schedule(tiles, groups, weights, finish):
    w_gate, w_up, w_down = weights
    bits = tensor_bits()
    token = None
    for kind, number in order_of(len(tiles)):
        tile = tiles[number]
        if kind == "up":
            coming = tiles[min(number + 1, len(tiles) - 1)].group
            rows, groups[coming] = after(token, groups[tile.group], groups[coming])
            tile.keep, send = project_up(rows, w_gate, w_up, tile.start, tile.width)
            token = tile.keep
            tile.arrived = xor_swap(send, "tensor", 1)
        elif kind == "fold":
            keep, arrived = after(token, tile.keep, tile.arrived)
            for bit in range(bits - 1):
                keep, send = fold(keep, arrived)
                arrived = xor_swap(send, "tensor", 2 << bit)
            tile.keep, tile.arrived = keep, arrived
            token = keep
        elif kind == "hidden":
            keep, arrived = after(token, tile.keep, tile.arrived)
            near = hidden(keep, arrived)
            token = near
            tile.pieces = [near]
            for bit in reversed(range(bits)):
                tile.pieces += [xor_swap(piece, "tensor", 1 << bit) for piece in tile.pieces]
        else:
            pieces = after(token, *tile.pieces)
            total = project_down(pieces, w_down, tile.start, tile.previous.out if tile.previous else None)
            token = total
            tile.out = total
            if tile.last:
                finish(tile.group, total)
    return token


def body(tokens, expert_ids, gate_probs, w_gate, w_up, w_down):
    tok_rows, feature_part = tokens.shape
    experts = lax.axis_size("expert")
    parts = lax.axis_size("tensor")
    bits = tensor_bits()
    capacity = 3 * tok_rows // experts
    piece = capacity // parts
    me = lax.axis_index("expert")
    my_part = lax.axis_index("tensor")

    relative = expert_ids ^ me
    names = relative[:, :, None] == jnp.arange(experts, dtype=jnp.int32)[None, None, :]
    named = jnp.any(names, axis=1)
    chance = jnp.sum(jnp.where(names, gate_probs[:, :, None], 0.0), axis=1)
    earlier = jnp.tril(jnp.ones((tok_rows, tok_rows), BF16), -1)
    rank = jnp.dot(earlier, named.astype(BF16), preferred_element_type=F32).astype(jnp.int32)
    place = jnp.where(named, rank, -1).T
    order = jnp.asarray([bit_reverse(j, bits) for j in range(parts)], jnp.int32) ^ my_part
    slots = (order[:, None] * piece + jnp.arange(piece, dtype=jnp.int32)[None, :]).reshape(-1)
    chosen = slots[None, :, None] == place[:, None, :]
    outgoing = jnp.dot(
        chosen.reshape(-1, tok_rows).astype(BF16), tokens, preferred_element_type=F32
    ).astype(BF16)
    outgoing = outgoing.reshape(experts, capacity, feature_part)

    members = [[0, 2], [3, 1] + list(range(4, experts))]
    arrived = {k: xor_swap(outgoing[k], "expert", k) if k else outgoing[k] for group in members for k in group}
    groups = []
    for group in members:
        rows = jnp.stack([arrived[k] for k in group]).reshape(len(group), parts, piece, feature_part)
        groups.append(rows.transpose(1, 0, 2, 3).reshape(-1, feature_part))
    unit = w_gate.shape[2] // 8
    tiles = []
    for group, cuts in enumerate(CUTS):
        start, previous = 0, None
        for cut in cuts:
            tile = Tile(group, start * unit, cut * unit, start + cut == 8)
            tile.previous = previous
            start, previous = start + cut, tile
            tiles.append(tile)

    sums = []

    def combine(k, rows):
        pick = chosen[k].astype(BF16)
        parts_of = [rows]
        if rows.dtype == F32:
            high = rows.astype(BF16)
            parts_of = [high, (rows - high.astype(F32)).astype(BF16)]
        picked = [
            lax.dot_general(pick, part, (((0,), (0,)), ((), ())), preferred_element_type=F32)
            for part in parts_of
        ]
        return sum(picked[1:], picked[0]) * chance[:, k][:, None]

    def finish(group, total):
        count = len(members[group])
        total = total.reshape(parts, count, piece, feature_part).transpose(1, 0, 2, 3)
        total = total.reshape(count, capacity, feature_part)
        for index, k in enumerate(members[group]):
            rows = total[index]
            if k:
                rows = xor_swap(rows.astype(BF16), "expert", k)
            sums.append(combine(k, rows))

    schedule(tiles, groups, (w_gate[0], w_up[0], w_down[0]), finish)
    mixed = sum(sums[1:], sums[0])
    size = lax.axis_size("fsdp")
    for bit in range(size.bit_length() - 1):
        mixed = mixed + xor_swap(mixed, "fsdp", 1 << bit)
    return mixed.astype(BF16)


def solution(mesh):
    return jax.shard_map(
        body,
        mesh=mesh,
        in_specs=(
            P("expert", "tensor"),
            P("expert", None),
            P("expert", None),
            P("expert", "tensor", "fsdp"),
            P("expert", "tensor", "fsdp"),
            P("expert", "fsdp", "tensor"),
        ),
        out_specs=P("expert", "tensor"),
        check_vma=False,
    )
```

```python
import functools

import jax
import jax.numpy as jnp
from jax import lax
from jax.experimental import pallas as pl
from jax.experimental.pallas import tpu as pltpu
from jax.sharding import PartitionSpec as P

F32 = jnp.float32
BF16 = jnp.bfloat16
VMEM_LIMIT = 24 * 1024 * 1024
SMALL_LIMIT = 14 * 1024 * 1024
BRIEF = pl.CostEstimate(flops=1, bytes_accessed=1, transcendentals=0)
LONG = pl.CostEstimate(flops=10**11, bytes_accessed=10**8, transcendentals=0)


def xor_swap(value, axis, distance):
    size = lax.axis_size(axis)
    return lax.ppermute(value, axis, [(i, i ^ distance) for i in range(size)])


def bit_reverse(value, bits):
    out = 0
    for _ in range(bits):
        out = out * 2 + value % 2
        value //= 2
    return out


def tile_width(width, options):
    for option in options:
        if width % option == 0:
            return option
    return None


def up_kernel(start, width, block, x_ref, gate_ref, up_ref, keep_ref, send_ref, weights, products, weight_sems, out_sems):
    half = x_ref.shape[0] // 2
    chunks = width // block
    depth = weights.shape[0]
    sources = (gate_ref, up_ref)

    def fetch(chunk, slot, which):
        columns = pl.ds(pl.multiple_of(start + chunk * block, block), block)
        return pltpu.make_async_copy(
            sources[which].at[:, columns], weights.at[slot, which], weight_sems.at[slot, which]
        )

    def store(chunk, slot, which, part):
        columns = pl.ds(pl.multiple_of(chunk * block, block), block)
        target = (keep_ref, send_ref)[part]
        return pltpu.make_async_copy(
            products.at[slot, which, pl.ds(part * half, half)],
            target.at[which, :, columns],
            out_sems.at[slot, which, part],
        )

    for chunk in range(min(depth, chunks)):
        for which in range(2):
            fetch(chunk, chunk, which).start()

    def step(chunk, carry):
        slot = lax.rem(chunk, depth)
        out_slot = lax.rem(chunk, 2)
        for which in range(2):
            fetch(chunk, slot, which).wait()

            @pl.when(chunk >= 2)
            def _():
                for part in range(2):
                    store(chunk - 2, out_slot, which, part).wait()

            products[out_slot, which] = jnp.dot(
                x_ref[...], weights[slot, which], preferred_element_type=F32
            )
            for part in range(2):
                store(chunk, out_slot, which, part).start()

            @pl.when(chunk + depth < chunks)
            def _():
                fetch(chunk + depth, slot, which).start()

        return carry

    lax.fori_loop(0, chunks, step, 0)
    for chunk in range(max(0, chunks - 2), chunks):
        for which in range(2):
            for part in range(2):
                store(chunk, chunk % 2, which, part).wait()


def project_up(rows, w_gate, w_up, start, width, cost):
    count, depth = rows.shape
    half = count // 2
    block = tile_width(width, (896, 512, 256))
    if half % 8 or count % 16 or depth % 128 or block is None or start % block:
        columns = slice(start, start + width)
        product = jnp.stack(
            [jnp.dot(rows, w[:, columns], preferred_element_type=F32) for w in (w_gate, w_up)]
        )
        return product[:, :half], product[:, half:]
    slots = min(4, width // block)
    anywhere = pl.BlockSpec(memory_space=pl.ANY)
    hbm = pl.BlockSpec(memory_space=pltpu.HBM)
    out_type = jax.ShapeDtypeStruct((2, half, width), F32)
    return pl.pallas_call(
        functools.partial(up_kernel, start, width, block),
        in_specs=[pl.BlockSpec(memory_space=pltpu.VMEM), hbm, hbm],
        out_specs=[anywhere, anywhere],
        out_shape=[out_type, out_type],
        scratch_shapes=[
            pltpu.VMEM((slots, 2, depth, block), BF16),
            pltpu.VMEM((2, 2, count, block), F32),
            pltpu.SemaphoreType.DMA((slots, 2)),
            pltpu.SemaphoreType.DMA((2, 2, 2)),
        ],
        compiler_params=pltpu.CompilerParams(vmem_limit_bytes=VMEM_LIMIT),
        cost_estimate=cost,
        name="project_up",
    )(rows, in_hbm(w_gate), in_hbm(w_up))


def down_kernel(start, width, block, count, has_total, *refs):
    pieces, w_ref = refs[:count], refs[count]
    out_ref, weights, sems = refs[-3:]
    chunks = width // block
    depth = weights.shape[0]

    def fetch(chunk, slot):
        rows = pl.ds(pl.multiple_of(start + chunk * block, block), block)
        return pltpu.make_async_copy(w_ref.at[rows], weights.at[slot], sems.at[slot])

    for chunk in range(min(depth, chunks)):
        fetch(chunk, chunk).start()
    out_ref[...] = refs[count + 1][...] if has_total else jnp.zeros_like(out_ref)

    def step(chunk, carry):
        slot = lax.rem(chunk, depth)
        fetch(chunk, slot).wait()
        columns = pl.ds(pl.multiple_of(chunk * block, block), block)
        hidden = [piece[:, columns] for piece in pieces]
        if pieces[0].shape[0] % 16:
            hidden = [piece.astype(F32) for piece in hidden]
        hidden = jnp.concatenate(hidden, axis=0).astype(BF16)
        out_ref[...] += jnp.dot(hidden, weights[slot], preferred_element_type=F32)

        @pl.when(chunk + depth < chunks)
        def _():
            fetch(chunk + depth, slot).start()

        return carry

    lax.fori_loop(0, chunks, step, 0)


def project_down(pieces, w_down, start, total, cost):
    rows, width = pieces[0].shape
    count = len(pieces)
    depth = w_down.shape[1]
    block = tile_width(width, (896, 512, 256))
    if rows % 8 or count * rows % 16 or depth % 128 or block is None or start % block:
        hidden = jnp.concatenate(pieces, axis=0)
        product = jnp.dot(hidden, w_down[start : start + width], preferred_element_type=F32)
        return product if total is None else total + product
    slots = min(6, width // block)
    vmem = pl.BlockSpec(memory_space=pltpu.VMEM)
    has_total = total is not None
    return pl.pallas_call(
        functools.partial(down_kernel, start, width, block, count, has_total),
        in_specs=[vmem] * count + [pl.BlockSpec(memory_space=pltpu.HBM)] + [vmem] * has_total,
        out_specs=vmem,
        out_shape=jax.ShapeDtypeStruct((count * rows, depth), F32),
        scratch_shapes=[
            pltpu.VMEM((slots, block, depth), BF16),
            pltpu.SemaphoreType.DMA((slots,)),
        ],
        compiler_params=pltpu.CompilerParams(vmem_limit_bytes=VMEM_LIMIT),
        cost_estimate=cost,
        name="project_down",
    )(*pieces, in_hbm(w_down), *([total] * has_total))


def fold_kernel(keep_ref, arrived_ref, kept_ref, send_ref):
    half, width = kept_ref.shape[1:]
    block = tile_width(width, (896, 512, 256))

    def step(chunk, carry):
        columns = pl.ds(pl.multiple_of(chunk * block, block), block)
        for which in range(2):
            total = keep_ref[which, :, columns] + arrived_ref[which, :, columns]
            kept_ref[which, :, columns] = total[:half]
            send_ref[which, :, columns] = total[half:].astype(BF16)
        return carry

    lax.fori_loop(0, width // block, step, 0)


def fold(keep, arrived):
    rows, width = keep.shape[1:]
    half = rows // 2
    if half % 8 or tile_width(width, (896, 512, 256)) is None or arrived.dtype != F32:
        total = keep + arrived.astype(F32)
        return total[:, :half], total[:, half:].astype(BF16)
    vmem = pl.BlockSpec(memory_space=pltpu.VMEM)
    return pl.pallas_call(
        fold_kernel,
        in_specs=[vmem, vmem],
        out_specs=[vmem, vmem],
        out_shape=[
            jax.ShapeDtypeStruct((2, half, width), F32),
            jax.ShapeDtypeStruct((2, half, width), BF16),
        ],
        compiler_params=pltpu.CompilerParams(vmem_limit_bytes=SMALL_LIMIT),
        cost_estimate=BRIEF,
        name="fold",
    )(keep, arrived)


def hidden_kernel(keep_ref, arrived_ref, out_ref):
    width = out_ref.shape[1]
    block = tile_width(width, (896, 512, 256))

    def step(chunk, carry):
        columns = pl.ds(pl.multiple_of(chunk * block, block), block)
        gate, up = [keep_ref[i, :, columns] + arrived_ref[i, :, columns].astype(F32) for i in range(2)]
        out_ref[:, columns] = (gate / (1.0 + jnp.exp(-gate)) * up).astype(BF16)
        return carry

    lax.fori_loop(0, width // block, step, 0)


def hidden(keep, arrived, cost):
    rows, width = keep.shape[1:]
    if rows % 8 or tile_width(width, (896, 512, 256)) is None:
        total = keep + arrived.astype(F32)
        return (jax.nn.silu(total[0]) * total[1]).astype(BF16)
    vmem = pl.BlockSpec(memory_space=pltpu.VMEM)
    return pl.pallas_call(
        hidden_kernel,
        in_specs=[vmem, vmem],
        out_specs=vmem,
        out_shape=jax.ShapeDtypeStruct((rows, width), BF16),
        compiler_params=pltpu.CompilerParams(vmem_limit_bytes=SMALL_LIMIT),
        cost_estimate=cost,
        name="hidden",
    )(keep, arrived)


def in_hbm(value):
    return pltpu.with_memory_space_constraint(value, pltpu.HBM)


def after(token, *values):
    if token is None:
        return values
    return lax.optimization_barrier((*values, token))[:-1]


def tensor_bits():
    return lax.axis_size("tensor").bit_length() - 1


class Tile:
    def __init__(self, group, start, width, last):
        self.group, self.start, self.width, self.last = group, start, width, last
        self.previous = None
        self.out = None


class Tile:
    def __init__(self, group, start, width):
        self.group, self.start, self.width = group, start, width


TILES = ((0, 0, 2), (0, 2, 2), (1, 0, 4), (1, 4, 4), (2, 4, 4), (3, 4, 4))
ORDER = (
    "U0 U1 f0 U2",
    "f1 h0 U3 f2",
    "h1 U4 d0 f3",
    "h2 d1 U5 f4",
    "h3 d2 f5 h4",
    "d3 d4 h5 z1",
    "d5",
)


def body(tokens, expert_ids, gate_probs, w_gate, w_up, w_down):
    tok_rows, feature_part = tokens.shape
    experts = lax.axis_size("expert")
    parts = lax.axis_size("tensor")
    bits = tensor_bits()
    capacity = 3 * tok_rows // experts
    piece = capacity // parts
    me = lax.axis_index("expert")
    my_part = lax.axis_index("tensor")

    relative = expert_ids ^ me
    names = relative[:, :, None] == jnp.arange(experts, dtype=jnp.int32)[None, None, :]
    named = jnp.any(names, axis=1)
    chance = jnp.sum(jnp.where(names, gate_probs[:, :, None], 0.0), axis=1)
    earlier = jnp.tril(jnp.ones((tok_rows, tok_rows), BF16), -1)
    rank = jnp.dot(earlier, named.astype(BF16), preferred_element_type=F32).astype(jnp.int32)
    place = jnp.where(named, rank, -1).T
    order = jnp.asarray([bit_reverse(j, bits) for j in range(parts)], jnp.int32) ^ my_part
    slots = (order[:, None] * piece + jnp.arange(piece, dtype=jnp.int32)[None, :]).reshape(-1)
    chosen = slots[None, :, None] == place[:, None, :]
    outgoing = jnp.dot(
        chosen.reshape(-1, tok_rows).astype(BF16), tokens, preferred_element_type=F32
    ).astype(BF16)
    outgoing = outgoing.reshape(experts, capacity, feature_part)

    def joined(blocks):
        rows = jnp.stack(blocks).reshape(len(blocks), parts, piece, -1)
        return rows.transpose(1, 0, 2, 3).reshape(len(blocks) * capacity, -1)

    def split(rows, count):
        rows = rows.reshape(parts, count, piece, -1).transpose(1, 0, 2, 3)
        return [block.reshape(capacity, -1) for block in rows]

    def combine(k, rows):
        pick = chosen[k].astype(BF16)
        parts_of = [rows]
        if rows.dtype == F32:
            high = rows.astype(BF16)
            parts_of = [high, (rows - high.astype(F32)).astype(BF16)]
        picked = [
            lax.dot_general(pick, part, (((0,), (0,)), ((), ())), preferred_element_type=F32)
            for part in parts_of
        ]
        return sum(picked[1:], picked[0]) * chance[:, k][:, None]

    arrived = [outgoing[0]] + [xor_swap(outgoing[k], "expert", k) for k in range(1, experts)]
    members = [[0, 1], list(range(2, experts)), [1], [0]]
    unit = w_gate.shape[2] // 8
    tiles = [Tile(group, start * unit, count * unit) for group, start, count in TILES]
    lasts = {tile.group: index for index, tile in enumerate(tiles)}
    rows_of, totals, back = {}, {}, {}
    token = None
    for step in " ".join(ORDER).split():
        kind, number = step[0].lower(), int(step[1:])
        cost = BRIEF if step[0].islower() else LONG
        tile = tiles[number]
        if kind == "u":
            if tile.group not in rows_of:
                blocks = after(token, *[arrived[k] for k in members[tile.group]])
                rows_of[tile.group] = joined(blocks)
            (rows,) = after(token, rows_of[tile.group])
            tile.keep, send = project_up(rows, w_gate[0], w_up[0], tile.start, tile.width, cost)
            token = tile.keep
            tile.arrived = xor_swap(send, "tensor", 1)
        elif kind == "f":
            keep, arrival = after(token, tile.keep, tile.arrived)
            for bit in range(bits - 1):
                keep, send = fold(keep, arrival)
                arrival = xor_swap(send, "tensor", 2 << bit)
            tile.keep, tile.arrived = keep, arrival
            token = keep
        elif kind == "h":
            keep, arrival = after(token, tile.keep, tile.arrived)
            near = hidden(keep, arrival, cost)
            token = near
            tile.pieces = [near]
            for bit in reversed(range(bits)):
                tile.pieces += [xor_swap(part, "tensor", 1 << bit) for part in tile.pieces]
        elif kind == "z":
            back[number] = after(token, *back[number])
        else:
            pieces = after(token, *tile.pieces)
            total = project_down(pieces, w_down[0], tile.start, totals.get(tile.group), cost)
            token = total
            totals[tile.group] = total
            if lasts[tile.group] == number:
                if tile.group == 0:
                    totals[3], totals[2] = split(total, 2)
                elif tile.group < 3:
                    blocks = split(total.astype(BF16), len(members[tile.group]))
                    back[tile.group] = [
                        xor_swap(block, "expert", k) for k, block in zip(members[tile.group], blocks)
                    ]
                else:
                    back[3] = [total]
    mixed = [combine(k, rows) for group in (1, 2, 3) for k, rows in zip(members[group], back[group])]
    mixed = sum(mixed[1:], mixed[0])
    size = lax.axis_size("fsdp")
    for bit in range(size.bit_length() - 1):
        rounded = mixed.astype(BF16)
        mixed = rounded.astype(F32) + xor_swap(rounded, "fsdp", 1 << bit).astype(F32)
    return mixed.astype(BF16)


def solution(mesh):
    return jax.shard_map(
        body,
        mesh=mesh,
        in_specs=(
            P("expert", "tensor"),
            P("expert", None),
            P("expert", None),
            P("expert", "tensor", "fsdp"),
            P("expert", "tensor", "fsdp"),
            P("expert", "fsdp", "tensor"),
        ),
        out_specs=P("expert", "tensor"),
        check_vma=False,
    )
```

```python
import functools

import jax
import jax.numpy as jnp
from jax import lax
from jax.experimental import pallas as pl
from jax.experimental.pallas import tpu as pltpu
from jax.sharding import PartitionSpec as P

F32 = jnp.float32
BF16 = jnp.bfloat16
VMEM_LIMIT = 24 * 1024 * 1024
SMALL_LIMIT = 14 * 1024 * 1024
BRIEF = pl.CostEstimate(flops=1, bytes_accessed=1, transcendentals=0)
LONG = pl.CostEstimate(flops=10**11, bytes_accessed=10**8, transcendentals=0)


def xor_swap(value, axis, distance):
    size = lax.axis_size(axis)
    return lax.ppermute(value, axis, [(i, i ^ distance) for i in range(size)])


def bit_reverse(value, bits):
    out = 0
    for _ in range(bits):
        out = out * 2 + value % 2
        value //= 2
    return out


def tile_width(width, options):
    for option in options:
        if width % option == 0:
            return option
    return None


def up_kernel(start, width, block, x_ref, gate_ref, up_ref, keep_ref, send_ref, weights, products, weight_sems, out_sems):
    half = x_ref.shape[0] // 2
    chunks = width // block
    depth = weights.shape[0]
    sources = (gate_ref, up_ref)

    def fetch(chunk, slot, which):
        columns = pl.ds(pl.multiple_of(start + chunk * block, block), block)
        return pltpu.make_async_copy(
            sources[which].at[:, columns], weights.at[slot, which], weight_sems.at[slot, which]
        )

    def store(chunk, slot, which, part):
        columns = pl.ds(pl.multiple_of(chunk * block, block), block)
        target = (keep_ref, send_ref)[part]
        return pltpu.make_async_copy(
            products.at[slot, which, pl.ds(part * half, half)],
            target.at[which, :, columns],
            out_sems.at[slot, which, part],
        )

    for chunk in range(min(depth, chunks)):
        for which in range(2):
            fetch(chunk, chunk, which).start()

    def step(chunk, carry):
        slot = lax.rem(chunk, depth)
        out_slot = lax.rem(chunk, 2)
        for which in range(2):
            fetch(chunk, slot, which).wait()

            @pl.when(chunk >= 2)
            def _():
                for part in range(2):
                    store(chunk - 2, out_slot, which, part).wait()

            products[out_slot, which] = jnp.dot(
                x_ref[...], weights[slot, which], preferred_element_type=F32
            )
            for part in range(2):
                store(chunk, out_slot, which, part).start()

            @pl.when(chunk + depth < chunks)
            def _():
                fetch(chunk + depth, slot, which).start()

        return carry

    lax.fori_loop(0, chunks, step, 0)
    for chunk in range(max(0, chunks - 2), chunks):
        for which in range(2):
            for part in range(2):
                store(chunk, chunk % 2, which, part).wait()


def project_up(rows, w_gate, w_up, start, width, cost):
    count, depth = rows.shape
    half = count // 2
    block = tile_width(width, (896, 512, 256))
    if half % 8 or count % 16 or depth % 128 or block is None or start % block:
        columns = slice(start, start + width)
        product = jnp.stack(
            [jnp.dot(rows, w[:, columns], preferred_element_type=F32) for w in (w_gate, w_up)]
        )
        return product[:, :half], product[:, half:]
    slots = min(4, width // block)
    anywhere = pl.BlockSpec(memory_space=pl.ANY)
    hbm = pl.BlockSpec(memory_space=pltpu.HBM)
    out_type = jax.ShapeDtypeStruct((2, half, width), F32)
    return pl.pallas_call(
        functools.partial(up_kernel, start, width, block),
        in_specs=[pl.BlockSpec(memory_space=pltpu.VMEM), hbm, hbm],
        out_specs=[anywhere, anywhere],
        out_shape=[out_type, out_type],
        scratch_shapes=[
            pltpu.VMEM((slots, 2, depth, block), BF16),
            pltpu.VMEM((2, 2, count, block), F32),
            pltpu.SemaphoreType.DMA((slots, 2)),
            pltpu.SemaphoreType.DMA((2, 2, 2)),
        ],
        compiler_params=pltpu.CompilerParams(vmem_limit_bytes=VMEM_LIMIT),
        cost_estimate=cost,
        name="project_up",
    )(rows, in_hbm(w_gate), in_hbm(w_up))


def down_kernel(start, width, block, count, has_total, *refs):
    pieces, w_ref = refs[:count], refs[count]
    out_ref, weights, sems = refs[-3:]
    chunks = width // block
    depth = weights.shape[0]

    def fetch(chunk, slot):
        rows = pl.ds(pl.multiple_of(start + chunk * block, block), block)
        return pltpu.make_async_copy(w_ref.at[rows], weights.at[slot], sems.at[slot])

    for chunk in range(min(depth, chunks)):
        fetch(chunk, chunk).start()
    out_ref[...] = refs[count + 1][...] if has_total else jnp.zeros_like(out_ref)

    def step(chunk, carry):
        slot = lax.rem(chunk, depth)
        fetch(chunk, slot).wait()
        columns = pl.ds(pl.multiple_of(chunk * block, block), block)
        hidden = [piece[:, columns] for piece in pieces]
        if pieces[0].shape[0] % 16:
            hidden = [piece.astype(F32) for piece in hidden]
        hidden = jnp.concatenate(hidden, axis=0).astype(BF16)
        out_ref[...] += jnp.dot(hidden, weights[slot], preferred_element_type=F32)

        @pl.when(chunk + depth < chunks)
        def _():
            fetch(chunk + depth, slot).start()

        return carry

    lax.fori_loop(0, chunks, step, 0)


def project_down(pieces, w_down, start, total, cost):
    rows, width = pieces[0].shape
    count = len(pieces)
    depth = w_down.shape[1]
    block = tile_width(width, (896, 512, 256))
    if rows % 8 or count * rows % 16 or depth % 128 or block is None or start % block:
        hidden = jnp.concatenate(pieces, axis=0)
        product = jnp.dot(hidden, w_down[start : start + width], preferred_element_type=F32)
        return product if total is None else total + product
    slots = min(6, width // block)
    vmem = pl.BlockSpec(memory_space=pltpu.VMEM)
    has_total = total is not None
    return pl.pallas_call(
        functools.partial(down_kernel, start, width, block, count, has_total),
        in_specs=[vmem] * count + [pl.BlockSpec(memory_space=pltpu.HBM)] + [vmem] * has_total,
        out_specs=vmem,
        out_shape=jax.ShapeDtypeStruct((count * rows, depth), F32),
        scratch_shapes=[
            pltpu.VMEM((slots, block, depth), BF16),
            pltpu.SemaphoreType.DMA((slots,)),
        ],
        compiler_params=pltpu.CompilerParams(vmem_limit_bytes=VMEM_LIMIT),
        cost_estimate=cost,
        name="project_down",
    )(*pieces, in_hbm(w_down), *([total] * has_total))


def fold_kernel(keep_ref, arrived_ref, kept_ref, send_ref):
    half, width = kept_ref.shape[1:]
    block = tile_width(width, (896, 512, 256))

    def step(chunk, carry):
        columns = pl.ds(pl.multiple_of(chunk * block, block), block)
        for which in range(2):
            total = keep_ref[which, :, columns] + arrived_ref[which, :, columns]
            kept_ref[which, :, columns] = total[:half]
            send_ref[which, :, columns] = total[half:].astype(BF16)
        return carry

    lax.fori_loop(0, width // block, step, 0)


def fold(keep, arrived):
    rows, width = keep.shape[1:]
    half = rows // 2
    if half % 8 or tile_width(width, (896, 512, 256)) is None or arrived.dtype != F32:
        total = keep + arrived.astype(F32)
        return total[:, :half], total[:, half:].astype(BF16)
    vmem = pl.BlockSpec(memory_space=pltpu.VMEM)
    return pl.pallas_call(
        fold_kernel,
        in_specs=[vmem, vmem],
        out_specs=[vmem, vmem],
        out_shape=[
            jax.ShapeDtypeStruct((2, half, width), F32),
            jax.ShapeDtypeStruct((2, half, width), BF16),
        ],
        compiler_params=pltpu.CompilerParams(vmem_limit_bytes=SMALL_LIMIT),
        cost_estimate=BRIEF,
        name="fold",
    )(keep, arrived)


def hidden_kernel(keep_ref, arrived_ref, out_ref):
    width = out_ref.shape[1]
    block = tile_width(width, (896, 512, 256))

    def step(chunk, carry):
        columns = pl.ds(pl.multiple_of(chunk * block, block), block)
        gate, up = [keep_ref[i, :, columns] + arrived_ref[i, :, columns].astype(F32) for i in range(2)]
        out_ref[:, columns] = (gate / (1.0 + jnp.exp(-gate)) * up).astype(BF16)
        return carry

    lax.fori_loop(0, width // block, step, 0)


def hidden(keep, arrived, cost):
    rows, width = keep.shape[1:]
    if rows % 8 or tile_width(width, (896, 512, 256)) is None:
        total = keep + arrived.astype(F32)
        return (jax.nn.silu(total[0]) * total[1]).astype(BF16)
    vmem = pl.BlockSpec(memory_space=pltpu.VMEM)
    return pl.pallas_call(
        hidden_kernel,
        in_specs=[vmem, vmem],
        out_specs=vmem,
        out_shape=jax.ShapeDtypeStruct((rows, width), BF16),
        compiler_params=pltpu.CompilerParams(vmem_limit_bytes=SMALL_LIMIT),
        cost_estimate=cost,
        name="hidden",
    )(keep, arrived)


def in_hbm(value):
    return pltpu.with_memory_space_constraint(value, pltpu.HBM)


def after(token, *values):
    if token is None:
        return values
    return lax.optimization_barrier((*values, token))[:-1]


def tensor_bits():
    return lax.axis_size("tensor").bit_length() - 1


class Tile:
    def __init__(self, group, start, width, last):
        self.group, self.start, self.width, self.last = group, start, width, last
        self.previous = None
        self.out = None


class Tile:
    def __init__(self, group, start, width):
        self.group, self.start, self.width = group, start, width


TILES = ((0, 0, 2), (0, 2, 2), (1, 0, 4), (1, 4, 4), (2, 4, 4), (3, 4, 4))
ORDER = (
    "U0 U1 f0 U2",
    "f1 h0 U3 f2",
    "h1 U4 d0 f3",
    "h2 d1 U5 f4",
    "h3 d2 f5 h4",
    "d3 d4 h5 d5",
)


def body(tokens, expert_ids, gate_probs, w_gate, w_up, w_down):
    tok_rows, feature_part = tokens.shape
    experts = lax.axis_size("expert")
    parts = lax.axis_size("tensor")
    bits = tensor_bits()
    capacity = 3 * tok_rows // experts
    piece = capacity // parts
    me = lax.axis_index("expert")
    my_part = lax.axis_index("tensor")

    relative = expert_ids ^ me
    names = relative[:, :, None] == jnp.arange(experts, dtype=jnp.int32)[None, None, :]
    named = jnp.any(names, axis=1)
    chance = jnp.sum(jnp.where(names, gate_probs[:, :, None], 0.0), axis=1)
    earlier = jnp.tril(jnp.ones((tok_rows, tok_rows), BF16), -1)
    rank = jnp.dot(earlier, named.astype(BF16), preferred_element_type=F32).astype(jnp.int32)
    place = jnp.where(named, rank, -1).T
    order = jnp.asarray([bit_reverse(j, bits) for j in range(parts)], jnp.int32) ^ my_part
    slots = (order[:, None] * piece + jnp.arange(piece, dtype=jnp.int32)[None, :]).reshape(-1)
    chosen = slots[None, :, None] == place[:, None, :]
    outgoing = jnp.dot(
        chosen.reshape(-1, tok_rows).astype(BF16), tokens, preferred_element_type=F32
    ).astype(BF16)
    outgoing = outgoing.reshape(experts, capacity, feature_part)

    def joined(blocks):
        rows = jnp.stack(blocks).reshape(len(blocks), parts, piece, -1)
        return rows.transpose(1, 0, 2, 3).reshape(len(blocks) * capacity, -1)

    def split(rows, count):
        rows = rows.reshape(parts, count, piece, -1).transpose(1, 0, 2, 3)
        return [block.reshape(capacity, -1) for block in rows]

    def combine(k, rows):
        pick = chosen[k].astype(BF16)
        parts_of = [rows]
        if rows.dtype == F32:
            high = rows.astype(BF16)
            parts_of = [high, (rows - high.astype(F32)).astype(BF16)]
        picked = [
            lax.dot_general(pick, part, (((0,), (0,)), ((), ())), preferred_element_type=F32)
            for part in parts_of
        ]
        return sum(picked[1:], picked[0]) * chance[:, k][:, None]

    arrived = [outgoing[0]] + [xor_swap(outgoing[k], "expert", k) for k in range(1, experts)]
    members = [[0, 1], list(range(2, experts)), [1], [0]]
    unit = w_gate.shape[2] // 8
    tiles = [Tile(group, start * unit, count * unit) for group, start, count in TILES]
    lasts = {tile.group: index for index, tile in enumerate(tiles)}
    rows_of, totals, back = {}, {}, {}
    token = None
    for step in " ".join(ORDER).split():
        kind, number = step[0].lower(), int(step[1:])
        cost = BRIEF if step[0].islower() else LONG
        tile = tiles[number]
        if kind == "u":
            if tile.group not in rows_of:
                blocks = after(token, *[arrived[k] for k in members[tile.group]])
                rows_of[tile.group] = joined(blocks)
            (rows,) = after(token, rows_of[tile.group])
            tile.keep, send = project_up(rows, w_gate[0], w_up[0], tile.start, tile.width, cost)
            token = tile.keep
            tile.arrived = xor_swap(send, "tensor", 1)
        elif kind == "f":
            keep, arrival = after(token, tile.keep, tile.arrived)
            for bit in range(bits - 1):
                keep, send = fold(keep, arrival)
                arrival = xor_swap(send, "tensor", 2 << bit)
            tile.keep, tile.arrived = keep, arrival
            token = keep
        elif kind == "h":
            keep, arrival = after(token, tile.keep, tile.arrived)
            near = hidden(keep, arrival, cost)
            token = near
            tile.pieces = [near]
            for bit in reversed(range(bits)):
                tile.pieces += [xor_swap(part, "tensor", 1 << bit) for part in tile.pieces]
        elif kind == "z":
            back[number] = after(token, *back[number])
        else:
            pieces = after(token, *tile.pieces)
            total = project_down(pieces, w_down[0], tile.start, totals.get(tile.group), cost)
            token = total
            totals[tile.group] = total
            if lasts[tile.group] == number:
                if tile.group == 0:
                    totals[3], totals[2] = split(total, 2)
                elif tile.group < 3:
                    blocks = split(total.astype(BF16), len(members[tile.group]))
                    back[tile.group] = [
                        xor_swap(block, "expert", k) for k, block in zip(members[tile.group], blocks)
                    ]
                else:
                    back[3] = [total]
    mixed = [combine(k, rows) for group in (1, 2, 3) for k, rows in zip(members[group], back[group])]
    mixed = sum(mixed[1:], mixed[0])
    size = lax.axis_size("fsdp")
    for bit in range(size.bit_length() - 1):
        rounded = mixed.astype(BF16)
        mixed = rounded.astype(F32) + xor_swap(rounded, "fsdp", 1 << bit).astype(F32)
    return mixed.astype(BF16)


def solution(mesh):
    return jax.shard_map(
        body,
        mesh=mesh,
        in_specs=(
            P("expert", "tensor"),
            P("expert", None),
            P("expert", None),
            P("expert", "tensor", "fsdp"),
            P("expert", "tensor", "fsdp"),
            P("expert", "fsdp", "tensor"),
        ),
        out_specs=P("expert", "tensor"),
        check_vma=False,
    )
```
